32 devices in a mesh: gx: 2 (over core), ha: 16 (over z, y, x).
Axes of the slice: x: 2, y: 2, z: 4, core: 2. Of those that a mesh axis runs over, the one named last changes fastest.
Arguments:
- level_set: float32 [48, 160, 256], P('ha', 'gx'), may hold values from -6 to 6
- step_length: float32 [1], replicated, may hold values from 0.12 to 0.2
Outputs:
- level_next: float32 [48, 160, 256], P('ha', 'gx')
The draws below stay inside these ranges and needn't reach their ends.
All inputs are finite; a program needn't handle non-finite values.
Results may differ from the reference program's by a relative error of at most 0.00002.
Values sent between devices are 32-bit elements; how exact they have to be, the bound alone decides.
A program may use at most 64 MiB of HBM per device.

```python
import jax
import jax.numpy as jnp
from jax import lax

CX = 3
NY = 256
NX = 48
NH = 160


def shard_levels(own_key, extent, split, smallest, largest):
    def one(dim, parts):
        heights = jax.random.uniform(jax.random.fold_in(jax.random.fold_in(own_key, 6), dim), (parts,), jnp.float32, smallest / len(split), largest / len(split))
        return jnp.repeat(jnp.exp(heights), extent[dim] // parts).reshape((-1,) + (1,) * (len(extent) - dim - 1))

    gain = one(*split[0])
    for cut in split[1:]:
        gain = gain * one(*cut)
    return gain


def noise(key, shape, deviation, limit, cuts=(), dtype=jnp.bfloat16):
    factor_of = shard_levels(key, shape, cuts, -0.22, 0.18) if cuts else 1.0
    array = jax.random.normal(key, shape, jnp.float32) * deviation * factor_of
    return jnp.minimum(jnp.maximum(array, -limit), limit).astype(dtype)


def setup_inputs(seed: int = 0) -> dict:
    splits = jax.random.split(jax.random.key(seed), 3)
    return {
        "level_set": noise(splits[0], (NX, NH, NY), 1.0, 6.0, ((0, 16), (1, 2)), jnp.float32),
        "step_length": jnp.clip(jax.random.uniform(splits[1], (1,), jnp.float32, 0.12, 0.2), 0.12, 0.2),
    }


epsilon_weno = 1e-6
speed_rate = 1.0
turn_rate = 1.0


def weno_blend(slope_one, slope_two, slope_three, slope_four, slope_five):
    guess_one = slope_one / 3.0 - 7.0 * slope_two / 6.0 + 11.0 * slope_three / 6.0
    guess_two = -slope_two / 6.0 + 5.0 * slope_three / 6.0 + slope_four / 3.0
    guess_three = slope_three / 3.0 + 5.0 * slope_four / 6.0 - slope_five / 6.0
    smooth_one = 13.0 / 12.0 * (slope_one - 2.0 * slope_two + slope_three) ** 2 + 0.25 * (slope_one - 4.0 * slope_two + 3.0 * slope_three) ** 2
    smooth_two = 13.0 / 12.0 * (slope_two - 2.0 * slope_three + slope_four) ** 2 + 0.25 * (slope_two - slope_four) ** 2
    smooth_three = 13.0 / 12.0 * (slope_three - 2.0 * slope_four + slope_five) ** 2 + 0.25 * (3.0 * slope_three - 4.0 * slope_four + slope_five) ** 2
    weight_one = 0.1 / (smooth_one + epsilon_weno) ** 2
    weight_two = 0.6 / (smooth_two + epsilon_weno) ** 2
    weight_three = 0.3 / (smooth_three + epsilon_weno) ** 2
    weight_sum = weight_one + weight_two + weight_three
    return (weight_one * guess_one + weight_two * guess_two + weight_three * guess_three) / weight_sum


def one_sided(padded, axis, count):
    forward_diff = lax.slice_in_dim(padded, 1, count + 6, axis=axis) - lax.slice_in_dim(padded, 0, count + 5, axis=axis)
    pieces = [lax.slice_in_dim(forward_diff, offset, offset + count, axis=axis) for offset in range(6)]
    minus_side = weno_blend(pieces[0], pieces[1], pieces[2], pieces[3], pieces[4])
    plus_side = weno_blend(pieces[5], pieces[4], pieces[3], pieces[2], pieces[1])
    return minus_side, plus_side


def hamilton_rate(padded, cosine_table, sine_table):
    rows_x = padded.shape[0] - 6
    rows_h = padded.shape[1] - 6
    rows_y = padded.shape[2] - 6
    minus_x, plus_x = one_sided(padded[:, 3:-3, 3:-3], 0, rows_x)
    minus_h, plus_h = one_sided(padded[3:-3, :, 3:-3], 1, rows_h)
    minus_y, plus_y = one_sided(padded[3:-3, 3:-3, :], 2, rows_y)
    cos_grid = cosine_table[None, :, None]
    sin_grid = sine_table[None, :, None]
    hamilton = speed_rate * (cos_grid * (minus_x + plus_x) * 0.5 + sin_grid * (minus_y + plus_y) * 0.5) - turn_rate * jnp.abs((minus_h + plus_h) * 0.5)
    damping = 0.5 * (speed_rate * jnp.abs(cos_grid) * (plus_x - minus_x) + speed_rate * jnp.abs(sin_grid) * (plus_y - minus_y) + turn_rate * (plus_h - minus_h))
    return damping - jnp.maximum(0.0, -hamilton)


def reference(level_set, step_length):
    step_size = step_length[0]
    heading = 2.0 * jnp.pi * jnp.arange(NH).astype(jnp.float32) / NH
    cosine_table = jnp.cos(heading)
    sine_table = jnp.sin(heading)

    def section_rate(section_field):
        padded = jnp.pad(section_field, ((3, 3), (0, 0), (3, 3)))
        padded = jnp.concatenate([padded[:, -3:], padded, padded[:, :3]], axis=1)

        def block_rate(number):
            slab_piece = lax.dynamic_slice_in_dim(padded, number * CX, CX + 6, 0)
            return hamilton_rate(slab_piece, cosine_table, sine_table)

        stacked = lax.map(block_rate, jnp.arange(NX // CX).astype(jnp.int32))
        return stacked.reshape(NX, NH, NY)

    section_one = level_set + step_size * section_rate(level_set)
    section_two = 0.75 * level_set + 0.25 * (section_one + step_size * section_rate(section_one))
    return level_set / 3.0 + (2.0 / 3.0) * (section_two + step_size * section_rate(section_two))
```

```python
import functools

import jax
import jax.numpy as jnp
import numpy as np
from jax import lax
from jax.experimental import pallas as pl
from jax.experimental.pallas import tpu as pltpu
from jax.sharding import PartitionSpec as P

MESH = pl.DeviceIdType.MESH
GROUP = 4
GHOST = 3
TILE = 8
LANES = 128
EPSILON = 4.0e-6 / 36.0
SMOOTH = 13.0 / 3.0


def quotient(top, bottom):
    return top / bottom


def indicator(slope, bend):
    whole = slope * slope + bend
    return whole * whole


def bent(second):
    return SMOOTH * (second * second) + EPSILON


def blend_both(d, ga, gb, gc, gd):
    sa, sb, sc = gb - ga, gc - gb, gd - gc
    m = gb + gc
    a = indicator(3.0 * gb - ga, bent(sa))
    b = indicator(m, bent(sb))
    c = indicator(3.0 * gc - gd, bent(sc))
    p, q, r = b * c, 6.0 * (a * c), a * b
    pt, rt = p * (sb - sa), r * (sc - sb)
    two = 2.0 * (pt + rt)
    left = d + m + gc - quotient(two + rt, p + q + 3.0 * r)
    right = d - m - gb + quotient(two + pt, 3.0 * p + q + r)
    return left, right


def differences(values):
    return [after - before for before, after in zip(values, values[1:])]


def sixths(values):
    return [(after - before) * (1.0 / 6.0) for before, after in zip(values, values[1:])]


def interface(u):
    d = differences(u)
    return blend_both(d[2], *sixths(d))


def kernel(sizes, step_ref, level_ref, trig_ref, out_ref, u_zero, u_one, u_two, last, in_send, in_recv, h_send, h_recv, x_send, x_recv, out_send, out_recv):
    block, rows, window, total_gx, total_ha = sizes
    layers = GROUP * block
    gx, ha = lax.axis_index("gx"), lax.axis_index("ha")
    team, pos = ha // GROUP, ha % GROUP

    def gray(n):
        return n + (n // 2) * (5 - 2 * n)

    def window_of(position):
        n = gray(position)
        return n + (gx % 2) * (GROUP - 1 - 2 * n)

    def position_of(number, core):
        return gray(number + (core % 2) * (GROUP - 1 - 2 * number))

    tiles, per = rows // TILE, window // TILE
    extra = tiles - GROUP * (per - 1)

    def start_of(number):
        after = (number + 1) * (per - 1) + jnp.minimum(number + 1, extra)
        return (after - per) * TILE

    w = window_of(pos)
    start = start_of(w)
    peers = [(pos + j) % GROUP for j in range(1, GROUP)]
    peer_ids = [(gx, team * GROUP + p) for p in peers]
    above_gx = (gx + (w + 1) // GROUP) % total_gx
    above_w = (w + 1) % GROUP
    above = (above_gx, team * GROUP + position_of(above_w, above_gx))
    below_gx = (gx + total_gx - (GROUP - w) // GROUP) % total_gx
    below_w = (w + GROUP - 1) % GROUP
    below = (below_gx, team * GROUP + position_of(below_w, below_gx))
    next_team, prior_team = (gx, ha + GROUP), (gx, ha - GROUP)
    has_next, has_prior = team < total_ha // GROUP - 1, team > 0

    rise = jnp.where(w == GROUP - 1, rows - start, start_of(above_w) - start)
    fall = jnp.where(w == 0, 0, start_of(below_w) + window - start)
    rise_row = pl.multiple_of(TILE + rise - TILE, TILE)
    fall_row = pl.multiple_of(TILE + fall, TILE)

    barrier = pltpu.get_barrier_semaphore()
    for device in peer_ids + [above, below]:
        pl.semaphore_signal(barrier, inc=1, device_id=device, device_id_type=MESH)

    @pl.when(has_next)
    def _():
        pl.semaphore_signal(barrier, inc=1, device_id=next_team, device_id_type=MESH)

    @pl.when(has_prior)
    def _():
        pl.semaphore_signal(barrier, inc=1, device_id=prior_team, device_id_type=MESH)

    @pl.when(jnp.logical_not(has_next))
    def _():
        for u in (u_zero, u_one, u_two):
            u[GHOST + layers :] = jnp.zeros((GHOST,) + u.shape[1:], jnp.float32)

    @pl.when(jnp.logical_not(has_prior))
    def _():
        for u in (u_zero, u_one, u_two):
            u[:GHOST] = jnp.zeros((GHOST,) + u.shape[1:], jnp.float32)

    own = pl.multiple_of(start, TILE)
    u_zero[pl.ds(GHOST + block * pos, block), TILE : TILE + window] = level_ref[:, pl.ds(own, window)]

    pl.semaphore_wait(barrier, GROUP + 1 + has_next.astype(jnp.int32) + has_prior.astype(jnp.int32))

    enter = []
    for j in range(GROUP - 1):
        there = pl.multiple_of(start_of(window_of(peers[j])), TILE)
        copy = pltpu.make_async_remote_copy(
            src_ref=level_ref.at[:, pl.ds(there, window)],
            dst_ref=u_zero.at[pl.ds(GHOST + block * pos, block), pl.ds(TILE, window)],
            send_sem=in_send.at[j],
            recv_sem=in_recv.at[j],
            device_id=peer_ids[j],
            device_id_type=MESH,
        )
        copy.start()
        enter.append(copy)
    for copy in enter:
        copy.wait_recv()

    spans = [(0, GHOST), (layers - GHOST, GHOST), (GHOST, layers - 2 * GHOST)]

    def heading_copies(stage, u, span):
        first, count = spans[span]
        where = pl.ds(GHOST + first, count)
        return [
            pltpu.make_async_remote_copy(
                src_ref=u.at[where, pl.ds(source, TILE)],
                dst_ref=u.at[where, pl.ds(target, TILE)],
                send_sem=h_send.at[stage, span, side],
                recv_sem=h_recv.at[stage, span, side],
                device_id=device,
                device_id_type=MESH,
            )
            for side, (source, target, device) in enumerate(
                [(rise_row, 0, above), (fall_row, TILE + window, below)]
            )
        ]

    def layer_copy(stage, u, side):
        source, target, device = [(GHOST, GHOST + layers, prior_team), (layers, 0, next_team)][side]
        return pltpu.make_async_remote_copy(
            src_ref=u.at[pl.ds(source, GHOST), pl.ds(TILE, window)],
            dst_ref=u.at[pl.ds(target, GHOST), pl.ds(TILE, window)],
            send_sem=x_send.at[stage, side],
            recv_sem=x_recv.at[stage, side],
            device_id=device,
            device_id_type=MESH,
        )

    def send_span(stage, u, span):
        if span == 0:
            pl.when(has_prior)(lambda: layer_copy(stage, u, 0).start())
        if span == 1:
            pl.when(has_next)(lambda: layer_copy(stage, u, 1).start())
        for copy in heading_copies(stage, u, span):
            copy.start()

    def await_span(stage, u, span):
        if span == 0:
            pl.when(has_prior)(lambda: layer_copy(stage, u, 1).wait_recv())
        if span == 1:
            pl.when(has_next)(lambda: layer_copy(stage, u, 0).wait_recv())
        for copy in heading_copies(stage, u, span):
            copy.wait_recv()

    lane = lax.broadcasted_iota(jnp.int32, (TILE, LANES), 1)
    halves = out_ref.shape[2] // LANES
    step_size = step_ref[0]
    turn = gx * rows + start

    def shifted(parts, by):
        turned = [pltpu.roll(part, (-by) % LANES, 1) for part in parts]
        if by < 0:
            return [jnp.where(lane < -by, before, here) for before, here in zip([0.0] + turned[:-1], turned)]
        return [jnp.where(lane >= LANES - by, after, here) for here, after in zip(turned, turned[1:] + [0.0])]

    def update(stage, u, target, span):
        first, count = spans[span]

        def tile_step(t, carry):
            row = pl.multiple_of(TILE + t * TILE, TILE)

            near = u.at[:, pl.ds(pl.multiple_of(t * TILE, TILE), 3 * TILE)]

            def cell(layer, half, off=0):
                return near[GHOST + layer, TILE + off : 2 * TILE + off, half * LANES : (half + 1) * LANES]

            cos_half = trig_ref[0, pl.ds(pl.multiple_of(turn + t * TILE, TILE), TILE)]
            sin_half = trig_ref[1, pl.ds(pl.multiple_of(turn + t * TILE, TILE), TILE)]

            ends = [jnp.zeros((TILE, LANES), jnp.float32) for _ in range(GHOST)]
            for n in range(count):
                tail = cell(first + n, halves - 1)
                for back in range(GHOST):
                    moved = pltpu.roll(tail, (GHOST - back + n) % LANES, 1)
                    ends[back] = jnp.where(lane == n, moved, ends[back])
            zero = jnp.zeros((TILE, LANES), jnp.float32)
            _, past = interface(ends + [zero] * 3)

            chain = []
            for half in range(halves):
                x_u = [cell(first + n, half) for n in range(-GHOST, count + GHOST)]
                x_d = differences(x_u)
                x_g = sixths(x_d)
                chain.append((x_d, x_g))
            left_x = [None] * halves
            for half in range(halves):
                x_d, x_g = chain[half]
                left_x[half], _ = blend_both(x_d[2], *x_g[0:4])
            for n in range(count):
                layer = first + n
                here = [cell(layer, half) for half in range(halves)]
                moved = {by: here if by == 0 else shifted(here, by) for by in range(-3, 3)}
                y_left, y_right = [], []
                for half in range(halves):
                    one, two = interface([moved[by][half] for by in range(-3, 3)])
                    y_left.append(one)
                    y_right.append(two)
                turned = [pltpu.roll(part, LANES - 1, 1) for part in y_right]
                turned.append(pltpu.roll(past, (LANES - 1 - n) % LANES, 1))
                y_right = [jnp.where(lane == LANES - 1, turned[i + 1], turned[i]) for i in range(halves)]
                for half in range(halves):
                    x_d, x_g = chain[half]
                    minus_x = left_x[half]
                    left_x[half], plus_x = blend_both(x_d[n + 3], *x_g[n + 1 : n + 5])
                    h_u = [here[half] if off == 0 else cell(layer, half, off) for off in range(-3, 4)]
                    minus_h, _ = interface(h_u[:6])
                    _, plus_h = interface(h_u[1:])
                    minus_y, plus_y = y_left[half], y_right[half]
                    hamilton = (
                        cos_half * (minus_x + plus_x) + sin_half * (minus_y + plus_y)
                    ) - 0.5 * jnp.abs(minus_h + plus_h)
                    rate = (
                        jnp.abs(cos_half) * (plus_x - minus_x)
                        + jnp.abs(sin_half) * (plus_y - minus_y)
                        + 0.5 * (plus_h - minus_h)
                        + jnp.minimum(hamilton, 0.0)
                    )
                    columns = slice(half * LANES, (half + 1) * LANES)
                    moved_on = here[half] + step_size * rate
                    if stage == 0:
                        u_one[GHOST + layer, pl.ds(row, TILE), columns] = moved_on
                    elif stage == 1:
                        base = u_zero[GHOST + layer, pl.ds(row, TILE), columns]
                        u_two[GHOST + layer, pl.ds(row, TILE), columns] = 0.75 * base + 0.25 * moved_on
                    else:
                        base = u_zero[GHOST + layer, pl.ds(row, TILE), columns]
                        last[layer, pl.ds(pl.multiple_of(t * TILE, TILE), TILE), columns] = (
                            base * (1.0 / 3.0) + (2.0 / 3.0) * moved_on
                        )
            return carry

        lax.fori_loop(0, per, tile_step, 0)

    def leave_copy(layer_pos, device, piece, slot):
        first, count = [(TILE, window - TILE), (0, TILE)][piece]
        return pltpu.make_async_remote_copy(
            src_ref=last.at[pl.ds(block * layer_pos, block), pl.ds(first, count)],
            dst_ref=out_ref.at[:, pl.ds(pl.multiple_of(start + first, TILE), count)],
            send_sem=out_send.at[piece, slot],
            recv_sem=out_recv.at[piece, slot],
            device_id=device,
            device_id_type=MESH,
        )

    fields = [u_zero, u_one, u_two]
    for span in range(3):
        send_span(0, u_zero, span)
    for stage in range(3):
        for span in range(3):
            await_span(stage, fields[stage], span)
            update(stage, fields[stage], None, span)
            if stage < 2:
                send_span(stage + 1, fields[stage + 1], span)

    whole = w < extra
    for j in range(GROUP - 1):
        leave_copy(peers[j], peer_ids[j], 0, j).start()
        pl.when(whole)(lambda: leave_copy(peers[j], peer_ids[j], 1, j).start())
    own_late = pl.multiple_of(start + TILE, TILE)
    out_ref[:, pl.ds(own_late, window - TILE)] = last[pl.ds(block * pos, block), TILE:]

    @pl.when(whole)
    def _():
        out_ref[:, pl.ds(own, TILE)] = last[pl.ds(block * pos, block), :TILE]

    for j in range(GROUP - 1):
        from_w = window_of((pos + GROUP - 1 - j) % GROUP)
        leave_copy(peers[j], peer_ids[j], 0, j).wait_recv()
        pl.when(from_w < extra)(lambda: leave_copy(peers[j], peer_ids[j], 1, j).wait_recv())
    for copy in enter:
        copy.wait_send()
    for stage in range(3):
        for span in range(3):
            for copy in heading_copies(stage, fields[stage], span):
                copy.wait_send()
        pl.when(has_prior)(lambda: layer_copy(stage, fields[stage], 0).wait_send())
        pl.when(has_next)(lambda: layer_copy(stage, fields[stage], 1).wait_send())
    for j in range(GROUP - 1):
        leave_copy(peers[j], peer_ids[j], 0, j).wait_send()
        pl.when(whole)(lambda: leave_copy(peers[j], peer_ids[j], 1, j).wait_send())


def on_device(level_set, step_length):
    block, rows, columns = level_set.shape
    total_gx, total_ha = lax.axis_size("gx"), lax.axis_size("ha")
    window = -(-(rows // TILE) // GROUP) * TILE
    angles = 2.0 * np.pi * np.arange(total_gx * rows) / (total_gx * rows)
    trig = np.stack([np.cos(angles), np.sin(angles)]) * 0.5
    trig = jnp.asarray(np.broadcast_to(trig[:, :, None], trig.shape + (LANES,)).astype(np.float32))
    field = pltpu.VMEM((GROUP * block + 2 * GHOST, window + 2 * TILE, columns), jnp.float32)
    dma = pltpu.SemaphoreType.DMA
    cells = block * rows * columns
    return pl.pallas_call(
        functools.partial(kernel, (block, rows, window, total_gx, total_ha)),
        out_shape=jax.ShapeDtypeStruct(level_set.shape, jnp.float32),
        in_specs=[
            pl.BlockSpec(memory_space=pltpu.SMEM),
            pl.BlockSpec(memory_space=pltpu.VMEM),
            pl.BlockSpec(memory_space=pltpu.VMEM),
        ],
        out_specs=pl.BlockSpec(memory_space=pltpu.VMEM),
        scratch_shapes=[
            field,
            field,
            field,
            pltpu.VMEM((GROUP * block, window, columns), jnp.float32),
            dma((GROUP - 1,)),
            dma((GROUP - 1,)),
            dma((3, 3, 2)),
            dma((3, 3, 2)),
            dma((3, 2)),
            dma((3, 2)),
            dma((2, GROUP - 1)),
            dma((2, GROUP - 1)),
        ],
        compiler_params=pltpu.CompilerParams(
            collective_id=0, has_side_effects=True, vmem_limit_bytes=32 * 1024 * 1024
        ),
        cost_estimate=pl.CostEstimate(flops=900 * cells, bytes_accessed=8 * cells, transcendentals=0),
    )(step_length, level_set, trig)


def solution(mesh):
    return jax.shard_map(
        on_device,
        mesh=mesh,
        in_specs=(P("ha", "gx", None), P()),
        out_specs=P("ha", "gx", None),
        check_vma=False,
    )
```

```python
import functools

import jax
import jax.numpy as jnp
import numpy as np
from jax import lax
from jax.experimental import pallas as pl
from jax.experimental.pallas import tpu as pltpu
from jax.sharding import PartitionSpec as P

MESH = pl.DeviceIdType.MESH
GROUP = 4
GHOST = 3
TILE = 8
LANES = 128
EPSILON = 4.0e-6 / 36.0
SMOOTH = 13.0 / 3.0


def quotient(top, bottom):
    return top / bottom


def indicator(slope, bend):
    whole = slope * slope + bend
    return whole * whole


def bent(second):
    return SMOOTH * (second * second) + EPSILON


def blend_both(d, ga, gb, gc, gd):
    sa, sb, sc = gb - ga, gc - gb, gd - gc
    m = gb + gc
    a = indicator(3.0 * gb - ga, bent(sa))
    b = indicator(m, bent(sb))
    c = indicator(3.0 * gc - gd, bent(sc))
    p, q, r = b * c, 6.0 * (a * c), a * b
    pt, rt = p * (sb - sa), r * (sc - sb)
    two = 2.0 * (pt + rt)
    left = d + m + gc - quotient(two + rt, p + q + 3.0 * r)
    right = d - m - gb + quotient(two + pt, 3.0 * p + q + r)
    return left, right


def differences(values):
    return [after - before for before, after in zip(values, values[1:])]


def sixths(values):
    return [(after - before) * (1.0 / 6.0) for before, after in zip(values, values[1:])]


def interface(u):
    d = differences(u)
    return blend_both(d[2], *sixths(d))


def kernel(sizes, step_ref, level_ref, trig_all, out_ref, u_zero, u_one, u_two, last, trig_ref, own_sem, in_send, in_recv, h_send, h_recv, x_send, x_recv, out_send, out_recv):
    block, rows, window, total_gx, total_ha = sizes
    layers = GROUP * block
    gx, ha = lax.axis_index("gx"), lax.axis_index("ha")
    team, pos = ha // GROUP, ha % GROUP

    def gray(n):
        return n + (n // 2) * (5 - 2 * n)

    def window_of(position):
        n = gray(position)
        return n + (gx % 2) * (GROUP - 1 - 2 * n)

    def position_of(number, core):
        return gray(number + (core % 2) * (GROUP - 1 - 2 * number))

    tiles, per = rows // TILE, window // TILE
    extra = tiles - GROUP * (per - 1)

    def start_of(number):
        after = (number + 1) * (per - 1) + jnp.minimum(number + 1, extra)
        return (after - per) * TILE

    w = window_of(pos)
    start = start_of(w)
    peers = [(pos + j) % GROUP for j in range(1, GROUP)]
    peer_ids = [(gx, team * GROUP + p) for p in peers]
    above_gx = (gx + (w + 1) // GROUP) % total_gx
    above_w = (w + 1) % GROUP
    above = (above_gx, team * GROUP + position_of(above_w, above_gx))
    below_gx = (gx + total_gx - (GROUP - w) // GROUP) % total_gx
    below_w = (w + GROUP - 1) % GROUP
    below = (below_gx, team * GROUP + position_of(below_w, below_gx))
    next_team, prior_team = (gx, ha + GROUP), (gx, ha - GROUP)
    has_next, has_prior = team < total_ha // GROUP - 1, team > 0

    rise = jnp.where(w == GROUP - 1, rows - start, start_of(above_w) - start)
    fall = jnp.where(w == 0, 0, start_of(below_w) + window - start)
    rise_row = pl.multiple_of(TILE + rise - TILE, TILE)
    fall_row = pl.multiple_of(TILE + fall, TILE)

    barrier = pltpu.get_barrier_semaphore()
    for device in peer_ids + [above, below]:
        pl.semaphore_signal(barrier, inc=1, device_id=device, device_id_type=MESH)

    @pl.when(has_next)
    def _():
        pl.semaphore_signal(barrier, inc=1, device_id=next_team, device_id_type=MESH)

    @pl.when(has_prior)
    def _():
        pl.semaphore_signal(barrier, inc=1, device_id=prior_team, device_id_type=MESH)

    @pl.when(jnp.logical_not(has_next))
    def _():
        for u in (u_zero, u_one, u_two):
            u[GHOST + layers :] = jnp.zeros((GHOST,) + u.shape[1:], jnp.float32)

    @pl.when(jnp.logical_not(has_prior))
    def _():
        for u in (u_zero, u_one, u_two):
            u[:GHOST] = jnp.zeros((GHOST,) + u.shape[1:], jnp.float32)

    own = pl.multiple_of(start, TILE)
    turn = pl.multiple_of(gx * rows + start, TILE)
    own_copy = pltpu.make_async_copy(
        level_ref.at[:, pl.ds(own, window)],
        u_zero.at[pl.ds(GHOST + block * pos, block), pl.ds(TILE, window)],
        own_sem.at[0],
    )
    own_copy.start()
    trig_copy = pltpu.make_async_copy(trig_all.at[:, pl.ds(turn, window)], trig_ref, own_sem.at[1])
    trig_copy.start()
    pl.semaphore_wait(barrier, GROUP + 1 + has_next.astype(jnp.int32) + has_prior.astype(jnp.int32))

    enter = []
    for j in range(GROUP - 1):
        there = pl.multiple_of(start_of(window_of(peers[j])), TILE)
        copy = pltpu.make_async_remote_copy(
            src_ref=level_ref.at[:, pl.ds(there, window)],
            dst_ref=u_zero.at[pl.ds(GHOST + block * pos, block), pl.ds(TILE, window)],
            send_sem=in_send.at[j],
            recv_sem=in_recv.at[j],
            device_id=peer_ids[j],
            device_id_type=MESH,
        )
        copy.start()
        enter.append(copy)

    def heading_copies(stage, u, span):
        where = pl.ds(GHOST + block * span, block)
        return [
            pltpu.make_async_remote_copy(
                src_ref=u.at[where, pl.ds(source, TILE)],
                dst_ref=u.at[where, pl.ds(target, TILE)],
                send_sem=h_send.at[stage, span, side],
                recv_sem=h_recv.at[stage, span, side],
                device_id=device,
                device_id_type=MESH,
            )
            for side, (source, target, device) in enumerate(
                [(rise_row, 0, above), (fall_row, TILE + window, below)]
            )
        ]

    def layer_copy(stage, u, side):
        source, target, device = [(GHOST, GHOST + layers, prior_team), (layers, 0, next_team)][side]
        return pltpu.make_async_remote_copy(
            src_ref=u.at[pl.ds(source, GHOST), pl.ds(TILE, window)],
            dst_ref=u.at[pl.ds(target, GHOST), pl.ds(TILE, window)],
            send_sem=x_send.at[stage, side],
            recv_sem=x_recv.at[stage, side],
            device_id=device,
            device_id_type=MESH,
        )

    def send_span(stage, u, span):
        pl.when((span == 0) & has_prior)(lambda: layer_copy(stage, u, 0).start())
        pl.when((span == GROUP - 1) & has_next)(lambda: layer_copy(stage, u, 1).start())
        for copy in heading_copies(stage, u, span):
            copy.start()

    def await_span(stage, u, span):
        if span == 0:
            pl.when(has_prior)(lambda: layer_copy(stage, u, 1).wait_recv())
        if span == GROUP - 1:
            pl.when(has_next)(lambda: layer_copy(stage, u, 0).wait_recv())
        for copy in heading_copies(stage, u, span):
            copy.wait_recv()

    lane = lax.broadcasted_iota(jnp.int32, (TILE, LANES), 1)
    halves = out_ref.shape[2] // LANES
    step_size = step_ref[0]

    def shifted(parts, by):
        turned = [pltpu.roll(part, (-by) % LANES, 1) for part in parts]
        if by < 0:
            return [jnp.where(lane < -by, before, here) for before, here in zip([0.0] + turned[:-1], turned)]
        return [jnp.where(lane >= LANES - by, after, here) for here, after in zip(turned, turned[1:] + [0.0])]

    def update(stage, u, target, span):
        first, count = block * span, block

        def tile_step(t, carry):
            row = pl.multiple_of(TILE + t * TILE, TILE)

            near = u.at[:, pl.ds(pl.multiple_of(t * TILE, TILE), 3 * TILE)]

            def cell(layer, half, off=0):
                return near[GHOST + layer, TILE + off : 2 * TILE + off, half * LANES : (half + 1) * LANES]

            cos_half = trig_ref[0, pl.ds(pl.multiple_of(t * TILE, TILE), TILE)]
            sin_half = trig_ref[1, pl.ds(pl.multiple_of(t * TILE, TILE), TILE)]

            ends = [jnp.zeros((TILE, LANES), jnp.float32) for _ in range(GHOST)]
            for n in range(count):
                tail = cell(first + n, halves - 1)
                for back in range(GHOST):
                    moved = pltpu.roll(tail, (GHOST - back + n) % LANES, 1)
                    ends[back] = jnp.where(lane == n, moved, ends[back])
            zero = jnp.zeros((TILE, LANES), jnp.float32)
            _, past = interface(ends + [zero] * 3)

            chain = []
            for half in range(halves):
                x_u = [cell(first + n, half) for n in range(-GHOST, count + GHOST)]
                x_d = differences(x_u)
                x_g = sixths(x_d)
                chain.append((x_d, x_g))
            left_x = [None] * halves
            for half in range(halves):
                x_d, x_g = chain[half]
                left_x[half], _ = blend_both(x_d[2], *x_g[0:4])
            for n in range(count):
                layer = first + n
                here = [cell(layer, half) for half in range(halves)]
                moved = {by: here if by == 0 else shifted(here, by) for by in range(-3, 3)}
                y_left, y_right = [], []
                for half in range(halves):
                    one, two = interface([moved[by][half] for by in range(-3, 3)])
                    y_left.append(one)
                    y_right.append(two)
                turned = [pltpu.roll(part, LANES - 1, 1) for part in y_right]
                turned.append(pltpu.roll(past, (LANES - 1 - n) % LANES, 1))
                y_right = [jnp.where(lane == LANES - 1, turned[i + 1], turned[i]) for i in range(halves)]
                for half in range(halves):
                    x_d, x_g = chain[half]
                    minus_x = left_x[half]
                    left_x[half], plus_x = blend_both(x_d[n + 3], *x_g[n + 1 : n + 5])
                    h_u = [here[half] if off == 0 else cell(layer, half, off) for off in range(-3, 4)]
                    minus_h, _ = interface(h_u[:6])
                    _, plus_h = interface(h_u[1:])
                    minus_y, plus_y = y_left[half], y_right[half]
                    hamilton = (
                        cos_half * (minus_x + plus_x) + sin_half * (minus_y + plus_y)
                    ) - 0.5 * jnp.abs(minus_h + plus_h)
                    rate = (
                        jnp.abs(cos_half) * (plus_x - minus_x)
                        + jnp.abs(sin_half) * (plus_y - minus_y)
                        + 0.5 * (plus_h - minus_h)
                        + jnp.minimum(hamilton, 0.0)
                    )
                    columns = slice(half * LANES, (half + 1) * LANES)
                    moved_on = here[half] + step_size * rate
                    if stage == 0:
                        u_one[GHOST + layer, pl.ds(row, TILE), columns] = moved_on
                    elif stage == 1:
                        base = u_zero[GHOST + layer, pl.ds(row, TILE), columns]
                        u_two[GHOST + layer, pl.ds(row, TILE), columns] = 0.75 * base + 0.25 * moved_on
                    else:
                        base = u_zero[GHOST + layer, pl.ds(row, TILE), columns]
                        last[layer, pl.ds(pl.multiple_of(t * TILE, TILE), TILE), columns] = (
                            base * (1.0 / 3.0) + (2.0 / 3.0) * moved_on
                        )
            return carry

        lax.fori_loop(0, per, tile_step, 0)

    def leave_copy(there, piece, sender):
        first, count = [(TILE, window - TILE), (0, TILE)][piece]
        return pltpu.make_async_remote_copy(
            src_ref=last.at[pl.ds(block * there, block), pl.ds(first, count)],
            dst_ref=out_ref.at[:, pl.ds(pl.multiple_of(start + first, TILE), count)],
            send_sem=out_send.at[piece, there],
            recv_sem=out_recv.at[piece, sender],
            device_id=(gx, team * GROUP + there),
            device_id_type=MESH,
        )

    whole = w < extra
    own_late = pl.multiple_of(start + TILE, TILE)

    def leave(there):
        @pl.when(pos != there)
        def _():
            leave_copy(there, 0, pos).start()
            pl.when(whole)(lambda: leave_copy(there, 1, pos).start())

        @pl.when(pos == there)
        def _():
            out_ref[:, pl.ds(own_late, window - TILE)] = last[block * there : block * (there + 1), TILE:]

            @pl.when(whole)
            def _():
                out_ref[:, pl.ds(own, TILE)] = last[block * there : block * (there + 1), :TILE]

    fields = [u_zero, u_one, u_two]
    own_copy.wait()
    send_span(0, u_zero, pos)
    for j in range(GROUP - 1):
        enter[j].wait_recv()
        send_span(0, u_zero, (pos + GROUP - 1 - j) % GROUP)
    trig_copy.wait()
    order = list(range(1, GROUP - 1)) + [0, GROUP - 1]
    for stage in range(3):
        for span in order:
            await_span(stage, fields[stage], span)
            update(stage, fields[stage], None, span)
            if stage < 2:
                send_span(stage + 1, fields[stage + 1], span)
            else:
                leave(span)

    for j in range(GROUP - 1):
        there = (pos + GROUP - 1 - j) % GROUP
        leave_copy(there, 0, there).wait_recv()
        pl.when(window_of(there) < extra)(lambda: leave_copy(there, 1, there).wait_recv())
    for copy in enter:
        copy.wait_send()
    for stage in range(3):
        for span in range(GROUP):
            for copy in heading_copies(stage, fields[stage], span):
                copy.wait_send()
        pl.when(has_prior)(lambda: layer_copy(stage, fields[stage], 0).wait_send())
        pl.when(has_next)(lambda: layer_copy(stage, fields[stage], 1).wait_send())
    for there in peers:
        leave_copy(there, 0, pos).wait_send()
        pl.when(whole)(lambda: leave_copy(there, 1, pos).wait_send())


def on_device(level_set, step_length):
    block, rows, columns = level_set.shape
    total_gx, total_ha = lax.axis_size("gx"), lax.axis_size("ha")
    window = -(-(rows // TILE) // GROUP) * TILE
    angles = 2.0 * np.pi * np.arange(total_gx * rows) / (total_gx * rows)
    trig = np.stack([np.cos(angles), np.sin(angles)]) * 0.5
    trig = jnp.asarray(np.broadcast_to(trig[:, :, None], trig.shape + (LANES,)).astype(np.float32))
    field = pltpu.VMEM((GROUP * block + 2 * GHOST, window + 2 * TILE, columns), jnp.float32)
    dma = pltpu.SemaphoreType.DMA
    cells = block * rows * columns
    return pl.pallas_call(
        functools.partial(kernel, (block, rows, window, total_gx, total_ha)),
        out_shape=jax.ShapeDtypeStruct(level_set.shape, jnp.float32),
        in_specs=[
            pl.BlockSpec(memory_space=pltpu.SMEM),
            pl.BlockSpec(memory_space=pltpu.HBM),
            pl.BlockSpec(memory_space=pltpu.HBM),
        ],
        out_specs=pl.BlockSpec(memory_space=pltpu.VMEM),
        scratch_shapes=[
            field,
            field,
            field,
            pltpu.VMEM((GROUP * block, window, columns), jnp.float32),
            pltpu.VMEM((2, window, LANES), jnp.float32),
            dma((2,)),
            dma((GROUP - 1,)),
            dma((GROUP - 1,)),
            dma((3, GROUP, 2)),
            dma((3, GROUP, 2)),
            dma((3, 2)),
            dma((3, 2)),
            dma((2, GROUP)),
            dma((2, GROUP)),
        ],
        compiler_params=pltpu.CompilerParams(
            collective_id=0, has_side_effects=True, vmem_limit_bytes=63 * 1024 * 1024
        ),
        cost_estimate=pl.CostEstimate(flops=900 * cells, bytes_accessed=8 * cells, transcendentals=0),
    )(step_length, level_set, trig)


def solution(mesh):
    return jax.shard_map(
        on_device,
        mesh=mesh,
        in_specs=(P("ha", "gx", None), P()),
        out_specs=P("ha", "gx", None),
        check_vma=False,
    )
```

```python
import functools

import jax
import jax.numpy as jnp
import numpy as np
from jax import lax
from jax.experimental import pallas as pl
from jax.experimental.pallas import tpu as pltpu
from jax.sharding import PartitionSpec as P

MESH = pl.DeviceIdType.MESH
GROUP = 4
GHOST = 3
TILE = 8
LANES = 128
EPSILON = 4.0e-6 / 36.0
SMOOTH = 13.0 / 3.0


def quotient(top, bottom):
    return top / bottom


def indicator(slope, bend):
    whole = slope * slope + bend
    return whole * whole


def bent(second):
    return SMOOTH * (second * second) + EPSILON


def blend_both(d, ga, gb, gc, gd):
    sa, sb, sc = gb - ga, gc - gb, gd - gc
    m = gb + gc
    a = indicator(3.0 * gb - ga, bent(sa))
    b = indicator(m, bent(sb))
    c = indicator(3.0 * gc - gd, bent(sc))
    p, q, r = b * c, 6.0 * (a * c), a * b
    pt, rt = p * (sb - sa), r * (sc - sb)
    two = 2.0 * (pt + rt)
    left = d + m + gc - quotient(two + rt, p + q + 3.0 * r)
    right = d - m - gb + quotient(two + pt, 3.0 * p + q + r)
    return left, right


def differences(values):
    return [after - before for before, after in zip(values, values[1:])]


def sixths(values):
    return [(after - before) * (1.0 / 6.0) for before, after in zip(values, values[1:])]


def interface(u):
    d = differences(u)
    return blend_both(d[2], *sixths(d))


def kernel(sizes, step_ref, level_ref, out_ref, u_zero, u_one, u_two, last, trig_ref, own_sem, in_send, in_recv, h_send, h_recv, x_send, x_recv, out_send, out_recv):
    block, rows, window, total_gx, total_ha = sizes
    layers = GROUP * block
    gx, ha = lax.axis_index("gx"), lax.axis_index("ha")
    team, pos = ha // GROUP, ha % GROUP

    def gray(n):
        return n + (n // 2) * (5 - 2 * n)

    def window_of(position):
        n = gray(position)
        return n + (gx % 2) * (GROUP - 1 - 2 * n)

    def position_of(number, core):
        return gray(number + (core % 2) * (GROUP - 1 - 2 * number))

    tiles, per = rows // TILE, window // TILE
    extra = tiles - GROUP * (per - 1)

    def start_of(number):
        after = (number + 1) * (per - 1) + jnp.minimum(number + 1, extra)
        return (after - per) * TILE

    w = window_of(pos)
    start = start_of(w)
    peers = [(pos + j) % GROUP for j in range(1, GROUP)]
    peer_ids = [(gx, team * GROUP + p) for p in peers]
    above_gx = (gx + (w + 1) // GROUP) % total_gx
    above_w = (w + 1) % GROUP
    above = (above_gx, team * GROUP + position_of(above_w, above_gx))
    below_gx = (gx + total_gx - (GROUP - w) // GROUP) % total_gx
    below_w = (w + GROUP - 1) % GROUP
    below = (below_gx, team * GROUP + position_of(below_w, below_gx))
    next_team, prior_team = (gx, ha + GROUP), (gx, ha - GROUP)
    has_next, has_prior = team < total_ha // GROUP - 1, team > 0

    rise = jnp.where(w == GROUP - 1, rows - start, start_of(above_w) - start)
    fall = jnp.where(w == 0, 0, start_of(below_w) + window - start)
    rise_row = pl.multiple_of(TILE + rise - TILE, TILE)
    fall_row = pl.multiple_of(TILE + fall, TILE)

    barrier = pltpu.get_barrier_semaphore()
    for device in peer_ids + [above, below]:
        pl.semaphore_signal(barrier, inc=1, device_id=device, device_id_type=MESH)

    @pl.when(has_next)
    def _():
        pl.semaphore_signal(barrier, inc=1, device_id=next_team, device_id_type=MESH)

    @pl.when(has_prior)
    def _():
        pl.semaphore_signal(barrier, inc=1, device_id=prior_team, device_id_type=MESH)

    @pl.when(jnp.logical_not(has_next))
    def _():
        for u in (u_zero, u_one, u_two):
            u[GHOST + layers :] = jnp.zeros((GHOST,) + u.shape[1:], jnp.float32)

    @pl.when(jnp.logical_not(has_prior))
    def _():
        for u in (u_zero, u_one, u_two):
            u[:GHOST] = jnp.zeros((GHOST,) + u.shape[1:], jnp.float32)

    own = pl.multiple_of(start, TILE)
    halves = out_ref.shape[2] // LANES

    def block_part(from_row, half):
        return (
            level_ref.at[:, pl.ds(from_row, window), pl.ds(half * LANES, LANES)],
            u_zero.at[pl.ds(GHOST + block * pos, block), half, pl.ds(TILE, window)],
        )

    own_copies = [pltpu.make_async_copy(*block_part(own, half), own_sem.at[half]) for half in range(halves)]
    for copy in own_copies:
        copy.start()
    pl.semaphore_wait(barrier, GROUP + 1 + has_next.astype(jnp.int32) + has_prior.astype(jnp.int32))

    enter = []
    for j in range(GROUP - 1):
        there = pl.multiple_of(start_of(window_of(peers[j])), TILE)
        for half in range(halves):
            source, target = block_part(there, half)
            copy = pltpu.make_async_remote_copy(
                src_ref=source,
                dst_ref=target,
                send_sem=in_send.at[j, half],
                recv_sem=in_recv.at[j, half],
                device_id=peer_ids[j],
                device_id_type=MESH,
            )
            copy.start()
            enter.append(copy)
    turn_cells = gx * rows + start + lax.broadcasted_iota(jnp.int32, (window, LANES), 0)
    heading = turn_cells.astype(jnp.float32) * (2.0 * np.pi / (total_gx * rows))
    trig_ref[0] = 0.5 * jnp.cos(heading)
    trig_ref[1] = 0.5 * jnp.sin(heading)

    def heading_copies(stage, u, span):
        where = pl.ds(GHOST + block * span, block)
        return [
            pltpu.make_async_remote_copy(
                src_ref=u.at[where, :, pl.ds(source, TILE)],
                dst_ref=u.at[where, :, pl.ds(target, TILE)],
                send_sem=h_send.at[stage, span, side],
                recv_sem=h_recv.at[stage, span, side],
                device_id=device,
                device_id_type=MESH,
            )
            for side, (source, target, device) in enumerate(
                [(rise_row, 0, above), (fall_row, TILE + window, below)]
            )
        ]

    def layer_copy(stage, u, side):
        source, target, device = [(GHOST, GHOST + layers, prior_team), (layers, 0, next_team)][side]
        return pltpu.make_async_remote_copy(
            src_ref=u.at[pl.ds(source, GHOST), :, pl.ds(TILE, window)],
            dst_ref=u.at[pl.ds(target, GHOST), :, pl.ds(TILE, window)],
            send_sem=x_send.at[stage, side],
            recv_sem=x_recv.at[stage, side],
            device_id=device,
            device_id_type=MESH,
        )

    def send_span(stage, u, span):
        pl.when((span == 0) & has_prior)(lambda: layer_copy(stage, u, 0).start())
        pl.when((span == GROUP - 1) & has_next)(lambda: layer_copy(stage, u, 1).start())
        for copy in heading_copies(stage, u, span):
            copy.start()

    def await_span(stage, u, span):
        if span == 0:
            pl.when(has_prior)(lambda: layer_copy(stage, u, 1).wait_recv())
        if span == GROUP - 1:
            pl.when(has_next)(lambda: layer_copy(stage, u, 0).wait_recv())
        for copy in heading_copies(stage, u, span):
            copy.wait_recv()

    lane = lax.broadcasted_iota(jnp.int32, (TILE, LANES), 1)
    step_size = step_ref[0]

    def shifted(parts, by):
        turned = [pltpu.roll(part, (-by) % LANES, 1) for part in parts]
        if by < 0:
            return [jnp.where(lane < -by, before, here) for before, here in zip([0.0] + turned[:-1], turned)]
        return [jnp.where(lane >= LANES - by, after, here) for here, after in zip(turned, turned[1:] + [0.0])]

    def update(stage, u, target, span):
        first, count = block * span, block

        def tile_step(t, carry):
            row = pl.multiple_of(TILE + t * TILE, TILE)

            near = u.at[:, :, pl.ds(pl.multiple_of(t * TILE, TILE), 3 * TILE)]

            def cell(layer, half, off=0):
                return near[GHOST + layer, half, TILE + off : 2 * TILE + off]

            cos_half = trig_ref[0, pl.ds(pl.multiple_of(t * TILE, TILE), TILE)]
            sin_half = trig_ref[1, pl.ds(pl.multiple_of(t * TILE, TILE), TILE)]

            ends = [jnp.zeros((TILE, LANES), jnp.float32) for _ in range(GHOST)]
            for n in range(count):
                tail = cell(first + n, halves - 1)
                for back in range(GHOST):
                    moved = pltpu.roll(tail, (GHOST - back + n) % LANES, 1)
                    ends[back] = jnp.where(lane == n, moved, ends[back])
            zero = jnp.zeros((TILE, LANES), jnp.float32)
            _, past = interface(ends + [zero] * 3)

            chain = []
            for half in range(halves):
                x_u = [cell(first + n, half) for n in range(-GHOST, count + GHOST)]
                x_d = differences(x_u)
                x_g = sixths(x_d)
                chain.append((x_d, x_g))
            left_x = [None] * halves
            for half in range(halves):
                x_d, x_g = chain[half]
                left_x[half], _ = blend_both(x_d[2], *x_g[0:4])
            for n in range(count):
                layer = first + n
                here = [cell(layer, half) for half in range(halves)]
                moved = {by: here if by == 0 else shifted(here, by) for by in range(-3, 3)}
                y_left, y_right = [], []
                for half in range(halves):
                    one, two = interface([moved[by][half] for by in range(-3, 3)])
                    y_left.append(one)
                    y_right.append(two)
                turned = [pltpu.roll(part, LANES - 1, 1) for part in y_right]
                turned.append(pltpu.roll(past, (LANES - 1 - n) % LANES, 1))
                y_right = [jnp.where(lane == LANES - 1, turned[i + 1], turned[i]) for i in range(halves)]
                for half in range(halves):
                    x_d, x_g = chain[half]
                    minus_x = left_x[half]
                    left_x[half], plus_x = blend_both(x_d[n + 3], *x_g[n + 1 : n + 5])
                    h_u = [here[half] if off == 0 else cell(layer, half, off) for off in range(-3, 4)]
                    minus_h, _ = interface(h_u[:6])
                    _, plus_h = interface(h_u[1:])
                    minus_y, plus_y = y_left[half], y_right[half]
                    hamilton = (
                        cos_half * (minus_x + plus_x) + sin_half * (minus_y + plus_y)
                    ) - 0.5 * jnp.abs(minus_h + plus_h)
                    rate = (
                        jnp.abs(cos_half) * (plus_x - minus_x)
                        + jnp.abs(sin_half) * (plus_y - minus_y)
                        + 0.5 * (plus_h - minus_h)
                        + jnp.minimum(hamilton, 0.0)
                    )
                    columns = slice(half * LANES, (half + 1) * LANES)
                    moved_on = here[half] + step_size * rate
                    if stage == 0:
                        u_one[GHOST + layer, half, pl.ds(row, TILE)] = moved_on
                    elif stage == 1:
                        base = u_zero[GHOST + layer, half, pl.ds(row, TILE)]
                        u_two[GHOST + layer, half, pl.ds(row, TILE)] = 0.75 * base + 0.25 * moved_on
                    else:
                        base = u_zero[GHOST + layer, half, pl.ds(row, TILE)]
                        last[layer, pl.ds(pl.multiple_of(t * TILE, TILE), TILE), columns] = (
                            base * (1.0 / 3.0) + (2.0 / 3.0) * moved_on
                        )
            return carry

        lax.fori_loop(0, per, tile_step, 0)

    def leave_copy(there, piece, sender):
        first, count = [(TILE, window - TILE), (0, TILE)][piece]
        return pltpu.make_async_remote_copy(
            src_ref=last.at[pl.ds(block * there, block), pl.ds(first, count)],
            dst_ref=out_ref.at[:, pl.ds(pl.multiple_of(start + first, TILE), count)],
            send_sem=out_send.at[piece, there],
            recv_sem=out_recv.at[piece, sender],
            device_id=(gx, team * GROUP + there),
            device_id_type=MESH,
        )

    whole = w < extra
    own_late = pl.multiple_of(start + TILE, TILE)

    def leave(there):
        @pl.when(pos != there)
        def _():
            leave_copy(there, 0, pos).start()
            pl.when(whole)(lambda: leave_copy(there, 1, pos).start())

        @pl.when(pos == there)
        def _():
            out_ref[:, pl.ds(own_late, window - TILE)] = last[block * there : block * (there + 1), TILE:]

            @pl.when(whole)
            def _():
                out_ref[:, pl.ds(own, TILE)] = last[block * there : block * (there + 1), :TILE]

    fields = [u_zero, u_one, u_two]
    for copy in own_copies:
        copy.wait()
    send_span(0, u_zero, pos)
    for j in range(GROUP - 1):
        for half in range(halves):
            enter[j * halves + half].wait_recv()
        send_span(0, u_zero, (pos + GROUP - 1 - j) % GROUP)
    order = list(range(1, GROUP - 1)) + [0, GROUP - 1]
    for stage in range(3):
        for span in order:
            await_span(stage, fields[stage], span)
            update(stage, fields[stage], None, span)
            if stage < 2:
                send_span(stage + 1, fields[stage + 1], span)
            else:
                leave(span)

    for j in range(GROUP - 1):
        there = (pos + GROUP - 1 - j) % GROUP
        leave_copy(there, 0, there).wait_recv()
        pl.when(window_of(there) < extra)(lambda: leave_copy(there, 1, there).wait_recv())
    for copy in enter:
        copy.wait_send()
    for stage in range(3):
        for span in range(GROUP):
            for copy in heading_copies(stage, fields[stage], span):
                copy.wait_send()
        pl.when(has_prior)(lambda: layer_copy(stage, fields[stage], 0).wait_send())
        pl.when(has_next)(lambda: layer_copy(stage, fields[stage], 1).wait_send())
    for there in peers:
        leave_copy(there, 0, pos).wait_send()
        pl.when(whole)(lambda: leave_copy(there, 1, pos).wait_send())


def on_device(level_set, step_length):
    block, rows, columns = level_set.shape
    total_gx, total_ha = lax.axis_size("gx"), lax.axis_size("ha")
    window = -(-(rows // TILE) // GROUP) * TILE
    halves = columns // LANES
    field = pltpu.VMEM((GROUP * block + 2 * GHOST, halves, window + 2 * TILE, LANES), jnp.float32)
    dma = pltpu.SemaphoreType.DMA
    cells = block * rows * columns
    return pl.pallas_call(
        functools.partial(kernel, (block, rows, window, total_gx, total_ha)),
        out_shape=jax.ShapeDtypeStruct(level_set.shape, jnp.float32),
        in_specs=[
            pl.BlockSpec(memory_space=pltpu.SMEM),
            pl.BlockSpec(memory_space=pltpu.HBM),
        ],
        out_specs=pl.BlockSpec(memory_space=pltpu.VMEM),
        scratch_shapes=[
            field,
            field,
            field,
            pltpu.VMEM((GROUP * block, window, columns), jnp.float32),
            pltpu.VMEM((2, window, LANES), jnp.float32),
            dma((halves,)),
            dma((GROUP - 1, halves)),
            dma((GROUP - 1, halves)),
            dma((3, GROUP, 2)),
            dma((3, GROUP, 2)),
            dma((3, 2)),
            dma((3, 2)),
            dma((2, GROUP)),
            dma((2, GROUP)),
        ],
        compiler_params=pltpu.CompilerParams(
            collective_id=0, has_side_effects=True, vmem_limit_bytes=32 * 1024 * 1024
        ),
        cost_estimate=pl.CostEstimate(flops=900 * cells, bytes_accessed=8 * cells, transcendentals=0),
    )(step_length, level_set)


def solution(mesh):
    return jax.shard_map(
        on_device,
        mesh=mesh,
        in_specs=(P("ha", "gx", None), P()),
        out_specs=P("ha", "gx", None),
        check_vma=False,
    )
```

```python
import functools

import jax
import jax.numpy as jnp
import numpy as np
from jax import lax
from jax.experimental import pallas as pl
from jax.experimental.pallas import tpu as pltpu
from jax.sharding import PartitionSpec as P

MESH = pl.DeviceIdType.MESH
GROUP = 4
GHOST = 3
TILE = 8
LANES = 128
EPSILON = 4.0e-6 / 36.0
SMOOTH = 13.0 / 3.0


def quotient(top, bottom):
    return top / bottom


def indicator(slope, bend):
    whole = slope * slope + bend
    return whole * whole


def bent(second):
    return SMOOTH * (second * second) + EPSILON


def blend_both(d, ga, gb, gc, gd):
    sa, sb, sc = gb - ga, gc - gb, gd - gc
    m = gb + gc
    a = indicator(3.0 * gb - ga, bent(sa))
    b = indicator(m, bent(sb))
    c = indicator(3.0 * gc - gd, bent(sc))
    p, q, r = b * c, 6.0 * (a * c), a * b
    pt, rt = p * (sb - sa), r * (sc - sb)
    two = 2.0 * (pt + rt)
    left = d + m + gc - quotient(two + rt, p + q + 3.0 * r)
    right = d - m - gb + quotient(two + pt, 3.0 * p + q + r)
    return left, right


def differences(values):
    return [after - before for before, after in zip(values, values[1:])]


def sixths(values):
    return [(after - before) * (1.0 / 6.0) for before, after in zip(values, values[1:])]


def interface(u):
    d = differences(u)
    return blend_both(d[2], *sixths(d))


def kernel(sizes, step_ref, level_ref, out_ref, u_zero, u_one, u_two, last, trig_ref, own_sem, in_send, in_recv, h_send, h_recv, x_send, x_recv, out_send, out_recv):
    block, rows, window, total_gx, total_ha = sizes
    layers = GROUP * block
    gx, ha = lax.axis_index("gx"), lax.axis_index("ha")
    team, pos = ha // GROUP, ha % GROUP

    def gray(n):
        return n + (n // 2) * (5 - 2 * n)

    def window_of(position):
        n = gray(position)
        return n + (gx % 2) * (GROUP - 1 - 2 * n)

    def position_of(number, core):
        return gray(number + (core % 2) * (GROUP - 1 - 2 * number))

    tiles, per = rows // TILE, window // TILE
    extra = tiles - GROUP * (per - 1)

    def start_of(number):
        after = (number + 1) * (per - 1) + jnp.minimum(number + 1, extra)
        return (after - per) * TILE

    w = window_of(pos)
    start = start_of(w)
    peers = [(pos + j) % GROUP for j in range(1, GROUP)]
    peer_ids = [(gx, team * GROUP + p) for p in peers]
    above_gx = (gx + (w + 1) // GROUP) % total_gx
    above_w = (w + 1) % GROUP
    above = (above_gx, team * GROUP + position_of(above_w, above_gx))
    below_gx = (gx + total_gx - (GROUP - w) // GROUP) % total_gx
    below_w = (w + GROUP - 1) % GROUP
    below = (below_gx, team * GROUP + position_of(below_w, below_gx))
    next_team, prior_team = (gx, ha + GROUP), (gx, ha - GROUP)
    has_next, has_prior = team < total_ha // GROUP - 1, team > 0

    rise = jnp.where(w == GROUP - 1, rows - start, start_of(above_w) - start)
    fall = jnp.where(w == 0, 0, start_of(below_w) + window - start)
    rise_row = pl.multiple_of(TILE + rise - TILE, TILE)
    fall_row = pl.multiple_of(TILE + fall, TILE)

    barrier = pltpu.get_barrier_semaphore()
    for device in peer_ids + [above, below]:
        pl.semaphore_signal(barrier, inc=1, device_id=device, device_id_type=MESH)

    @pl.when(has_next)
    def _():
        pl.semaphore_signal(barrier, inc=1, device_id=next_team, device_id_type=MESH)

    @pl.when(has_prior)
    def _():
        pl.semaphore_signal(barrier, inc=1, device_id=prior_team, device_id_type=MESH)

    @pl.when(jnp.logical_not(has_next))
    def _():
        for u in (u_zero, u_one, u_two):
            u[GHOST + layers :] = jnp.zeros((GHOST,) + u.shape[1:], jnp.float32)

    @pl.when(jnp.logical_not(has_prior))
    def _():
        for u in (u_zero, u_one, u_two):
            u[:GHOST] = jnp.zeros((GHOST,) + u.shape[1:], jnp.float32)

    own = pl.multiple_of(start, TILE)
    halves = out_ref.shape[2] // LANES

    def block_part(from_row, half):
        return (
            level_ref.at[:, pl.ds(from_row, window), pl.ds(half * LANES, LANES)],
            u_zero.at[pl.ds(GHOST + block * pos, block), half, pl.ds(TILE, window)],
        )

    own_copies = [pltpu.make_async_copy(*block_part(own, half), own_sem.at[half]) for half in range(halves)]
    for copy in own_copies:
        copy.start()
    pl.semaphore_wait(barrier, GROUP + 1 + has_next.astype(jnp.int32) + has_prior.astype(jnp.int32))

    enter = []
    for j in range(GROUP - 1):
        there = pl.multiple_of(start_of(window_of(peers[j])), TILE)
        for half in range(halves):
            source, target = block_part(there, half)
            copy = pltpu.make_async_remote_copy(
                src_ref=source,
                dst_ref=target,
                send_sem=in_send.at[j, half],
                recv_sem=in_recv.at[j, half],
                device_id=peer_ids[j],
                device_id_type=MESH,
            )
            copy.start()
            enter.append(copy)
    turn_cells = gx * rows + start + lax.broadcasted_iota(jnp.int32, (window, LANES), 0)
    heading = turn_cells.astype(jnp.float32) * (2.0 * np.pi / (total_gx * rows))
    trig_ref[0] = 0.5 * jnp.cos(heading)
    trig_ref[1] = 0.5 * jnp.sin(heading)

    def heading_copies(stage, u, span):
        where = pl.ds(GHOST + block * span, block)
        return [
            pltpu.make_async_remote_copy(
                src_ref=u.at[where, :, pl.ds(source, TILE)],
                dst_ref=u.at[where, :, pl.ds(target, TILE)],
                send_sem=h_send.at[stage, span, side],
                recv_sem=h_recv.at[stage, span, side],
                device_id=device,
                device_id_type=MESH,
            )
            for side, (source, target, device) in enumerate(
                [(rise_row, 0, above), (fall_row, TILE + window, below)]
            )
        ]

    def layer_copy(stage, u, side):
        source, target, device = [(GHOST, GHOST + layers, prior_team), (layers, 0, next_team)][side]
        return pltpu.make_async_remote_copy(
            src_ref=u.at[pl.ds(source, GHOST), :, pl.ds(TILE, window)],
            dst_ref=u.at[pl.ds(target, GHOST), :, pl.ds(TILE, window)],
            send_sem=x_send.at[stage, side],
            recv_sem=x_recv.at[stage, side],
            device_id=device,
            device_id_type=MESH,
        )

    def send_span(stage, u, span):
        pl.when((span == 0) & has_prior)(lambda: layer_copy(stage, u, 0).start())
        pl.when((span == GROUP - 1) & has_next)(lambda: layer_copy(stage, u, 1).start())
        for copy in heading_copies(stage, u, span):
            copy.start()

    def await_span(stage, u, span):
        if span == 0:
            pl.when(has_prior)(lambda: layer_copy(stage, u, 1).wait_recv())
        if span == GROUP - 1:
            pl.when(has_next)(lambda: layer_copy(stage, u, 0).wait_recv())
        for copy in heading_copies(stage, u, span):
            copy.wait_recv()

    lane = lax.broadcasted_iota(jnp.int32, (TILE, LANES), 1)
    step_size = step_ref[0]

    def shifted(parts, by):
        turned = [pltpu.roll(part, (-by) % LANES, 1) for part in parts]
        if by < 0:
            return [jnp.where(lane < -by, before, here) for before, here in zip([0.0] + turned[:-1], turned)]
        return [jnp.where(lane >= LANES - by, after, here) for here, after in zip(turned, turned[1:] + [0.0])]

    def update(stage, u, target, span):
        first, count = block * span, block

        def tile_step(t, carry):
            row = pl.multiple_of(TILE + t * TILE, TILE)

            near = u.at[:, :, pl.ds(pl.multiple_of(t * TILE, TILE), 3 * TILE)]

            def cell(layer, half, off=0):
                return near[GHOST + layer, half, TILE + off : 2 * TILE + off]

            cos_half = trig_ref[0, pl.ds(pl.multiple_of(t * TILE, TILE), TILE)]
            sin_half = trig_ref[1, pl.ds(pl.multiple_of(t * TILE, TILE), TILE)]

            ends = [jnp.zeros((TILE, LANES), jnp.float32) for _ in range(GHOST)]
            for n in range(count):
                tail = cell(first + n, halves - 1)
                for back in range(GHOST):
                    moved = pltpu.roll(tail, (GHOST - back + n) % LANES, 1)
                    ends[back] = jnp.where(lane == n, moved, ends[back])
            zero = jnp.zeros((TILE, LANES), jnp.float32)
            _, past = interface(ends + [zero] * 3)

            chain = []
            for half in range(halves):
                x_u = [cell(first + n, half) for n in range(-GHOST, count + GHOST)]
                x_d = differences(x_u)
                x_g = sixths(x_d)
                chain.append((x_d, x_g))
            left_x = [None] * halves
            for half in range(halves):
                x_d, x_g = chain[half]
                left_x[half], _ = blend_both(x_d[2], *x_g[0:4])
            for n in range(count):
                layer = first + n
                here = [cell(layer, half) for half in range(halves)]
                moved = {by: here if by == 0 else shifted(here, by) for by in range(-3, 3)}
                y_left, y_right = [], []
                for half in range(halves):
                    one, two = interface([moved[by][half] for by in range(-3, 3)])
                    y_left.append(one)
                    y_right.append(two)
                turned = [pltpu.roll(part, LANES - 1, 1) for part in y_right]
                turned.append(pltpu.roll(past, (LANES - 1 - n) % LANES, 1))
                y_right = [jnp.where(lane == LANES - 1, turned[i + 1], turned[i]) for i in range(halves)]
                for half in range(halves):
                    x_d, x_g = chain[half]
                    minus_x = left_x[half]
                    left_x[half], plus_x = blend_both(x_d[n + 3], *x_g[n + 1 : n + 5])
                    h_u = [here[half] if off == 0 else cell(layer, half, off) for off in range(-3, 4)]
                    minus_h, _ = interface(h_u[:6])
                    _, plus_h = interface(h_u[1:])
                    minus_y, plus_y = y_left[half], y_right[half]
                    hamilton = (
                        cos_half * (minus_x + plus_x) + sin_half * (minus_y + plus_y)
                    ) - 0.5 * jnp.abs(minus_h + plus_h)
                    rate = (
                        jnp.abs(cos_half) * (plus_x - minus_x)
                        + jnp.abs(sin_half) * (plus_y - minus_y)
                        + 0.5 * (plus_h - minus_h)
                        + jnp.minimum(hamilton, 0.0)
                    )
                    columns = slice(half * LANES, (half + 1) * LANES)
                    moved_on = here[half] + step_size * rate
                    if stage == 0:
                        u_one[GHOST + layer, half, pl.ds(row, TILE)] = moved_on
                    elif stage == 1:
                        base = u_zero[GHOST + layer, half, pl.ds(row, TILE)]
                        u_two[GHOST + layer, half, pl.ds(row, TILE)] = 0.75 * base + 0.25 * moved_on
                    else:
                        base = u_zero[GHOST + layer, half, pl.ds(row, TILE)]
                        last[layer, pl.ds(pl.multiple_of(t * TILE, TILE), TILE), columns] = (
                            base * (1.0 / 3.0) + (2.0 / 3.0) * moved_on
                        )
            return carry

        lax.fori_loop(0, per, tile_step, 0, unroll=True)

    def leave_copy(there, piece, sender):
        first, count = [(TILE, window - TILE), (0, TILE)][piece]
        return pltpu.make_async_remote_copy(
            src_ref=last.at[pl.ds(block * there, block), pl.ds(first, count)],
            dst_ref=out_ref.at[:, pl.ds(pl.multiple_of(start + first, TILE), count)],
            send_sem=out_send.at[piece, there],
            recv_sem=out_recv.at[piece, sender],
            device_id=(gx, team * GROUP + there),
            device_id_type=MESH,
        )

    whole = w < extra
    own_late = pl.multiple_of(start + TILE, TILE)

    def leave(there):
        @pl.when(pos != there)
        def _():
            leave_copy(there, 0, pos).start()
            pl.when(whole)(lambda: leave_copy(there, 1, pos).start())

        @pl.when(pos == there)
        def _():
            out_ref[:, pl.ds(own_late, window - TILE)] = last[block * there : block * (there + 1), TILE:]

            @pl.when(whole)
            def _():
                out_ref[:, pl.ds(own, TILE)] = last[block * there : block * (there + 1), :TILE]

    fields = [u_zero, u_one, u_two]
    for copy in own_copies:
        copy.wait()
    send_span(0, u_zero, pos)
    for j in range(GROUP - 1):
        for half in range(halves):
            enter[j * halves + half].wait_recv()
        send_span(0, u_zero, (pos + GROUP - 1 - j) % GROUP)
    order = list(range(1, GROUP - 1)) + [0, GROUP - 1]
    for stage in range(3):
        for span in order:
            await_span(stage, fields[stage], span)
            update(stage, fields[stage], None, span)
            if stage < 2:
                send_span(stage + 1, fields[stage + 1], span)
            else:
                leave(span)

    for j in range(GROUP - 1):
        there = (pos + GROUP - 1 - j) % GROUP
        leave_copy(there, 0, there).wait_recv()
        pl.when(window_of(there) < extra)(lambda: leave_copy(there, 1, there).wait_recv())
    for copy in enter:
        copy.wait_send()
    for stage in range(3):
        for span in range(GROUP):
            for copy in heading_copies(stage, fields[stage], span):
                copy.wait_send()
        pl.when(has_prior)(lambda: layer_copy(stage, fields[stage], 0).wait_send())
        pl.when(has_next)(lambda: layer_copy(stage, fields[stage], 1).wait_send())
    for there in peers:
        leave_copy(there, 0, pos).wait_send()
        pl.when(whole)(lambda: leave_copy(there, 1, pos).wait_send())


def on_device(level_set, step_length):
    block, rows, columns = level_set.shape
    total_gx, total_ha = lax.axis_size("gx"), lax.axis_size("ha")
    window = -(-(rows // TILE) // GROUP) * TILE
    halves = columns // LANES
    field = pltpu.VMEM((GROUP * block + 2 * GHOST, halves, window + 2 * TILE, LANES), jnp.float32)
    dma = pltpu.SemaphoreType.DMA
    cells = block * rows * columns
    return pl.pallas_call(
        functools.partial(kernel, (block, rows, window, total_gx, total_ha)),
        out_shape=jax.ShapeDtypeStruct(level_set.shape, jnp.float32),
        in_specs=[
            pl.BlockSpec(memory_space=pltpu.SMEM),
            pl.BlockSpec(memory_space=pltpu.HBM),
        ],
        out_specs=pl.BlockSpec(memory_space=pltpu.VMEM),
        scratch_shapes=[
            field,
            field,
            field,
            pltpu.VMEM((GROUP * block, window, columns), jnp.float32),
            pltpu.VMEM((2, window, LANES), jnp.float32),
            dma((halves,)),
            dma((GROUP - 1, halves)),
            dma((GROUP - 1, halves)),
            dma((3, GROUP, 2)),
            dma((3, GROUP, 2)),
            dma((3, 2)),
            dma((3, 2)),
            dma((2, GROUP)),
            dma((2, GROUP)),
        ],
        compiler_params=pltpu.CompilerParams(
            collective_id=0, has_side_effects=True, vmem_limit_bytes=32 * 1024 * 1024
        ),
        cost_estimate=pl.CostEstimate(flops=900 * cells, bytes_accessed=8 * cells, transcendentals=0),
    )(step_length, level_set)


def solution(mesh):
    return jax.shard_map(
        on_device,
        mesh=mesh,
        in_specs=(P("ha", "gx", None), P()),
        out_specs=P("ha", "gx", None),
        check_vma=False,
    )
```
